256 devices in a mesh: section: 8 (over x, core), tensor: 8 (over z), ctx: 4 (over y).
Axes of the slice: x: 4, y: 4, z: 8, core: 2. Of those that a mesh axis runs over, the one named last changes fastest.
Arguments:
- hidden: bfloat16 [1024, 8192], P(('section', 'tensor'), 'ctx'), may hold values from -20 to 20
- head_weight: bfloat16 [8192, 65536], P('ctx', ('section', 'tensor')), may hold values from -1 to 1
- target_ids: int32 [1024], P('ctx'), may hold values from 0 to 65535
- seq_ids: int32 [1024], P('ctx'), may hold values from 0 to 3, as said below
- response_mask: int32 [1024], P('ctx'), may hold values from 0 to 1
- ref_means: float32 [4], replicated, may hold values from -12.5 to -10.5
Outputs:
- target_logprobs: float32 [1024], P('ctx')
- logit_grad: bfloat16 [1024, 65536], P('ctx', ('section', 'tensor'))
- weight_grad: bfloat16 [8192, 65536], P('ctx', ('section', 'tensor'))
- hidden_grad: bfloat16 [1024, 8192], P(('section', 'tensor'), 'ctx')
The draws below stay inside these ranges and needn't reach their ends.
Inputs may be any that keep to these rules, and one draw needn't show every extreme that they name: `seq_ids`: never falls along the tokens; every sequence has at least one position.
All inputs are finite; a program needn't handle non-finite values.
Results may differ from the reference program's by a relative error of at most 0.001.
The reference program's roundings to bfloat16 on the way count: a program that leaves them out, or rounds other values in their place, can miss the bound.
Values may be sent and summed in bfloat16 or wider, within the bound.
A program may use at most 64 MiB of HBM per device.

```python
import jax
import jax.numpy as jnp
from jax import lax

D = 8192
VOC_DEV = 1024
PAIRS = 2
TOKENS = 1024
VOCAB = 65536


def hidden_base(key, spread):
    values = jnp.clip(jax.random.normal(jax.random.fold_in(key, 7), (TOKENS, D), jnp.float32), -6.0, 6.0)
    scales = jnp.exp(jax.random.uniform(jax.random.fold_in(key, 8), (TOKENS, 1), jnp.float32, -spread, spread))
    return values * scales


def sequence_layout(key):
    sequence_count = 2 * PAIRS
    short_length = jax.random.randint(jax.random.fold_in(key, 11), (), 1, 5, dtype=jnp.int32)
    short_seq = 1 + 2 * jax.random.randint(jax.random.fold_in(key, 12), (), 0, PAIRS, dtype=jnp.int32)
    spans = TOKENS // 8 + jax.random.randint(jax.random.fold_in(key, 13), (sequence_count - 2,), 0, TOKENS // 4, dtype=jnp.int32)
    remainder = TOKENS - short_length - jnp.sum(spans)
    others = jnp.concatenate([spans, remainder[None]])
    seq_index = jnp.arange(sequence_count, dtype=jnp.int32)
    slot_index = jnp.clip(seq_index - (seq_index > short_seq).astype(jnp.int32), 0, sequence_count - 2)
    lengths = jnp.where(seq_index == short_seq, short_length, jnp.take(others, slot_index))
    ends = jnp.cumsum(lengths).astype(jnp.int32)
    positions = jnp.arange(TOKENS, dtype=jnp.int32)
    sequences = jnp.sum((positions[:, None] >= ends[None, :sequence_count - 1]).astype(jnp.int32), axis=1).astype(jnp.int32)
    return (sequences, short_seq)


def draw_seq_ids(key, part):
    sequences, short_seq = sequence_layout(key)
    return sequences


def draw_response_mask(key, part):
    sequences, short_seq = sequence_layout(key)
    key = jax.random.fold_in(key, 22)
    keep = jax.random.randint(key, (TOKENS,), 0, 4, dtype=jnp.int32) < 3
    return (keep & (sequences != short_seq)).astype(jnp.int32)


def draw_hidden(key, part):
    return hidden_base(key, 0.0).astype(jnp.bfloat16)


def draw_head_weight(key, part):
    own_key = jax.random.fold_in(key, 5)
    weight = jnp.clip(jax.random.normal(own_key, (D, VOCAB), jnp.float32), -6.0, 6.0) * D ** (-0.5)
    return weight.astype(jnp.bfloat16)


def place_ends(values, stream_key, least, top_value):
    index_at = [jax.random.randint(jax.random.fold_in(stream_key, axis), (), 0, length) for axis, length in enumerate(values.shape)]
    longest = values.shape.index(max(values.shape))
    neighbour = index_at[:longest] + [(index_at[longest] + 1) % values.shape[longest]] + index_at[longest + 1:]
    return values.at[tuple(index_at)].set(least).at[tuple(neighbour)].set(top_value)


def setup_inputs(seed: int = 0) -> dict:
    keys = jax.random.split(jax.random.key(seed), 7)
    hidden = draw_hidden(jax.random.fold_in(keys[6], 71), 0)
    head_weight = draw_head_weight(jax.random.fold_in(keys[6], 71), 0)
    target_ids = place_ends(jax.random.randint(keys[2], (TOKENS,), 0, VOCAB), jax.random.fold_in(keys[2], 1), 0, VOCAB - 1).astype(jnp.int32)
    seq_ids = draw_seq_ids(jax.random.fold_in(keys[6], 71), 0)
    response_mask = draw_response_mask(jax.random.fold_in(keys[6], 71), 0)
    ref_means = jnp.clip(jax.random.uniform(keys[5], (2 * PAIRS,), jnp.float32, -12.5, -10.5), -12.5, -10.5)
    return {"hidden": hidden, "head_weight": head_weight, "target_ids": target_ids, "seq_ids": seq_ids, "response_mask": response_mask, "ref_means": ref_means}


beta_scale = 2.0
loss_scale = 1024.0


def reference(hidden, head_weight, target_ids, seq_ids, response_mask, ref_means):
    logits = jnp.dot(hidden, head_weight, preferred_element_type=jnp.float32)
    row_top = jnp.max(logits, axis=1)
    row_total = jnp.sum(jnp.exp(logits - row_top[:, None]), axis=1)
    target_logit = jnp.take_along_axis(logits, target_ids[:, None], axis=1)[:, 0]
    logprob = target_logit - row_top - jnp.log(row_total)
    sequence_count = 2 * PAIRS
    membership = (seq_ids[:, None] == jnp.arange(sequence_count, dtype=jnp.int32)[None, :]).astype(jnp.float32)
    membership = membership * response_mask.astype(jnp.float32)[:, None]
    counts = jnp.maximum(jnp.sum(membership, axis=0), 1.0)
    seq_means = jnp.sum(membership * logprob[:, None], axis=0) / counts
    pair_diffs = (seq_means - ref_means).reshape(PAIRS, 2)
    margin = beta_scale * (pair_diffs[:, 0] - pair_diffs[:, 1])
    chosen_push = -(loss_scale / PAIRS) * beta_scale * (1.0 - jax.nn.sigmoid(margin))
    seq_grad = jnp.stack([chosen_push, -chosen_push], axis=1).reshape(sequence_count) / counts
    token_coef = jnp.sum(membership * seq_grad[None, :], axis=1)
    softmax = jnp.exp(logits - row_top[:, None]) / row_total[:, None]
    target_hit = (lax.broadcasted_iota(jnp.int32, logits.shape, 1) == target_ids[:, None]).astype(jnp.float32)
    logit_grad = (token_coef[:, None] * (target_hit - softmax)).astype(jnp.bfloat16)
    blocks = logit_grad.reshape(TOKENS, VOCAB // VOC_DEV, VOC_DEV).transpose(1, 0, 2)
    weight_blocks = lax.map(lambda piece_grad: jnp.dot(hidden.T, piece_grad, preferred_element_type=jnp.float32).astype(jnp.bfloat16), blocks)
    weight_grad = weight_blocks.transpose(1, 0, 2).reshape(D, VOCAB)
    hidden_grad = lax.dot_general(logit_grad, head_weight, (((1,), (1,)), ((), ())), preferred_element_type=jnp.float32).astype(jnp.bfloat16)
    return logprob, logit_grad, weight_grad, hidden_grad
```

```python
import functools

import jax
import jax.numpy as jnp
from jax import lax
from jax.experimental import pallas as pl
from jax.experimental.pallas import tpu as pltpu
from jax.sharding import PartitionSpec as P

MESH = pl.DeviceIdType.MESH
beta_scale = 2.0
loss_scale = 1024.0
ROWS = 16
NX, NY, NZ = 4, 4, 8
WA, WB, WZ = 768, 512, 384
F32, BF16 = jnp.float32, jnp.bfloat16

AHEAD = 2

TURNED = 0


def flip(v):
    return v + 1 - 2 * lax.rem(v, 2)


def mirror(v):
    return 3 - v


def across(v):
    return lax.rem(v + 2, 4)


def kernel(
    hid_hbm, w_hbm, tgt_ref, seq_ref, msk_ref, rm_ref,
    lp_out, lg_out, wg_out, hg_out,
    hid, w, wt, part, r1, r2, ex, cs, tc, cc,
    st1, st2, st3, ga, gsib, hg_a, hg_b, hg_z, xa1, xb1, xa2, xb2,
    zo, zr_r, zr_l, zz_r, zz_l, xz1, xz2, wst,
    loc_sem, x_s, x_r, z_s, z_r, sib_s, sib_r, ws_s, ws_r,
    y1_s, y1_r, y2_s, y2_r, a_s, a_r, b_s, b_r, c_s, c_r,
    g_s, g_r, gb_s, gb_r, x1_s, x1_r, x2_s, x2_r, cr_s, cr_r, cl_s, cl_r,
    dr_s, dr_r, dl_s, dl_r, e1_s, e1_r, e2_s, e2_r, out_sem,
):
    s = lax.axis_index("section")
    z = lax.axis_index("tensor")
    y = lax.axis_index("ctx")
    x, k = lax.div(s, 2), lax.rem(s, 2)
    width, vocab = w.shape
    sib = {"section": 2 * x + 1 - k}
    z_right, z_left = {"tensor": lax.rem(z + 1, NZ)}, {"tensor": lax.rem(z + NZ - 1, NZ)}
    sends = []

    def send(src, dst, ssem, rsem, device):
        copy = pltpu.make_async_remote_copy(
            src_ref=src, dst_ref=dst, send_sem=ssem, recv_sem=rsem,
            device_id=device, device_id_type=MESH,
        )
        copy.start()
        sends.append(copy)
        return copy

    w_load = pltpu.make_async_copy(w_hbm, w, loc_sem.at[0])
    w_load.start()
    h_load = pltpu.make_async_copy(hid_hbm, hid.at[z, x, k], loc_sem.at[1])
    h_load.start()

    def transpose_weight(i):
        cols = slice(i * 256, (i + 1) * 256)
        wt[0:vocab, cols] = w[cols, :].T

    barrier = pltpu.get_barrier_semaphore()
    peers = [{"section": lax.rem(s + d, 8)} for d in range(1, 8)]
    peers += [{"tensor": lax.rem(z + d, NZ)} for d in range(1, NZ)]
    peers += [{"ctx": lax.rem(y + d, NY)} for d in range(1, NY)]
    for peer in peers:
        pl.semaphore_signal(barrier, inc=1, device_id=peer, device_id_type=MESH)
    w_load.wait()
    for i in range(TURNED):
        transpose_weight(i)
    pl.semaphore_wait(barrier, len(peers))

    def zm(d):
        return lax.rem(z + d + NZ, NZ)

    order = [0, -1, 1, -2, 2, -3, 3, 4]
    x_copies, z_copies, sib_copies = {}, {}, {}

    def x_send(o):
        zc = zm(order[o])
        src = hid.at[zc, x, k] if o else hid_hbm
        x_copies[o] = [
            send(src, hid.at[zc, x, k], x_s.at[o, d - 1], x_r.at[o, d - 1],
                 {"section": 2 * lax.rem(x + d, NX) + k})
            for d in range(1, NX)
        ]

    def z_send(o):
        z_copies[o] = send(
            hid_hbm, hid.at[z, x, k], z_s.at[o - 1], z_r.at[o - 1], {"tensor": zm(-order[o])})

    def sib_send(o):
        for copy in x_copies[o]:
            copy.wait_recv()
        block = hid.at[zm(order[o]), :, k]
        sib_copies[o] = send(block, block, sib_s.at[o], sib_r.at[o], sib)

    x_send(0)
    for o in range(1, 3):
        z_send(o)

    tc[...] = jnp.broadcast_to(tgt_ref[...].astype(F32), (128, 2 * 128)).T
    offset = ((s * NZ + z) * vocab).astype(F32)

    def hits(rows):
        lanes = lax.broadcasted_iota(jnp.int32, (ROWS, vocab), 1).astype(F32) + offset
        return lanes == tc[rows, 0:1]

    def rows_of(zc, kk):
        return pl.ds(pl.multiple_of(kk * 128 + zc * ROWS, ROWS), ROWS)

    def chunk(zc):
        for p in range(2):
            a = hid[zc].reshape(NX * 2 * ROWS, width)
            r = jnp.dot(a, w[:, p * 512 : (p + 1) * 512], preferred_element_type=F32)
            part[zc, p] = r.reshape(NY, 2, ROWS, 512)

    y1 = {}
    y2 = {}

    def y1_send(o, zc):
        for slot in (1, 0):
            for p, partner in ((0, flip(y)), (1, mirror(y))):
                quarter = across(y) if slot else partner
                y1[o, p, slot] = send(
                    part.at[zc, p, quarter], r1.at[zc, p, slot],
                    y1_s.at[o, p, slot], y1_r.at[o, p, slot], {"ctx": partner})

    def y1_take(o, zc):
        for p, partner in ((0, mirror(y)), (1, flip(y))):
            y1[o, p, 1].wait_recv()
            r1[zc, p, 1] = r1[zc, p, 1] + part[zc, p, partner]
            y2[o, p] = send(
                r1.at[zc, p, 1], r2.at[zc, p], y2_s.at[o, p], y2_r.at[o, p], {"ctx": partner})

    def y2_take(o, zc):
        for p in range(2):
            y1[o, p, 0].wait_recv()
            y2[o, p].wait_recv()
        lane = lax.broadcasted_iota(jnp.int32, (ROWS, 128), 1)
        for kk in range(2):
            rows = rows_of(zc, kk)
            l = jnp.concatenate(
                [part[zc, p, y, kk] + r1[zc, p, 0, kk] + r2[zc, p, kk] for p in range(2)], axis=1)
            top = jnp.max(l, axis=1, keepdims=True)
            e = jnp.exp(l - top)
            ex[zc, kk] = e
            total = jnp.sum(e, axis=1, keepdims=True)
            target = jnp.sum(jnp.where(hits(rows), l, 0.0), axis=1, keepdims=True)
            cs[rows, :] = jnp.where(lane == 0, top, jnp.where(lane == 1, total, target))

    h_load.wait()
    sib_send(0)
    z_copies[1].wait_recv()
    x_send(1)
    z_send(3)
    for o in range(NZ):
        if o + 2 < NZ:
            z_copies[o + 2].wait_recv()
            x_send(o + 2)
            if o + 4 < NZ:
                z_send(o + 4)
        sib_copies[o].wait_recv()
        chunk(zm(order[o]))
        y1_send(o, zm(order[o]))
        if o + 1 < NZ:
            sib_send(o + 1)
        if o >= 1:
            y1_take(o - 1, zm(order[o - 1]))
        if 1 <= o <= 4:
            for i in range(TURNED + (8 - TURNED) * (o - 1) // 4, TURNED + (8 - TURNED) * o // 4):
                transpose_weight(i)
        if o == 4:
            w_copy = send(
                wt.at[pl.ds(0, vocab)], wt.at[pl.ds(vocab, vocab)], ws_s, ws_r, sib)
        if o >= 3:
            y2_take(o - 3, zm(order[o - 3]))
    y1_take(7, zm(order[7]))
    for o in range(5, 8):
        y2_take(o, zm(order[o]))

    st1[s] = cs[...].T[0:8]
    a_copies = [
        send(st1.at[s], st1.at[s], a_s.at[d - 1], a_r.at[d - 1], {"section": lax.rem(s + d, 8)})
        for d in range(1, 8)
    ]
    for copy in a_copies:
        copy.wait_recv()

    row = lax.broadcasted_iota(jnp.int32, (8, 256), 0)

    def combine(buf):
        top = buf[0, 0:1]
        for i in range(1, 8):
            top = jnp.maximum(top, buf[i, 0:1])
        total = jnp.zeros_like(top)
        target = jnp.zeros_like(top)
        for i in range(8):
            total = total + buf[i, 1:2] * jnp.exp(buf[i, 0:1] - top)
            target = target + buf[i, 2:3]
        return top, total, target

    top, total, target = combine(st1)
    st2[z] = jnp.where(row == 0, top, jnp.where(row == 1, total, target))
    b_copies = [
        send(st2.at[z], st2.at[z], b_s.at[d - 1], b_r.at[d - 1], {"tensor": lax.rem(z + d, NZ)})
        for d in range(1, NZ)
    ]
    for copy in b_copies:
        copy.wait_recv()
    top, total, target = combine(st2)
    logprob = target - top - jnp.log(total)
    lp_out[...] = logprob
    scale = jnp.exp(st1[s, 0:1] - top) / total

    mask = msk_ref[...].astype(F32)
    members = [jnp.where(seq_ref[...] == i, mask, 0.0) for i in range(4)]
    lane = lax.broadcasted_iota(jnp.int32, (8, 128), 1)
    sums = jnp.zeros((8, 128), F32)
    for i in range(4):
        sums = jnp.where(lane == i, jnp.sum(members[i] * logprob, axis=1, keepdims=True), sums)
        sums = jnp.where(lane == 4 + i, jnp.sum(members[i], axis=1, keepdims=True), sums)
    st3[y] = sums
    c_copies = [
        send(st3.at[y], st3.at[y], c_s.at[d - 1], c_r.at[d - 1], {"ctx": lax.rem(y + d, NY)})
        for d in range(1, NY)
    ]
    for copy in c_copies:
        copy.wait_recv()
    sums = st3[0] + st3[1] + st3[2] + st3[3]

    def pick(i):
        return jnp.sum(jnp.where(lane == i, sums, 0.0), axis=1, keepdims=True)[0:1]

    counts = [jnp.maximum(pick(4 + i), 1.0) for i in range(4)]
    diffs = [pick(i) / counts[i] - rm_ref[i] for i in range(4)]
    coef = jnp.zeros((1, 256), F32)
    for pair in range(2):
        margin = beta_scale * (diffs[2 * pair] - diffs[2 * pair + 1])
        push = -(loss_scale / 2) * beta_scale * (1.0 - jax.nn.sigmoid(margin))
        coef = coef + members[2 * pair] * (push / counts[2 * pair])
        coef = coef + members[2 * pair + 1] * (-push / counts[2 * pair + 1])
    wide = lax.broadcasted_iota(jnp.int32, (128, 256), 0)
    cc[...] = jnp.where(wide == 0, coef, scale).T

    pairs = [(zm(3 - j), zm(4 + j - NZ)) for j in range(4)]
    y_right, y_left = lax.rem(y + 1, NY), lax.rem(y + NY - 1, NY)
    g = {}

    def gather_send(j):
        for t in range(2):
            block = ga.at[pairs[j][t], y]
            for d, to in enumerate((y_right, y_left)):
                g[j, t, d] = send(
                    block, block, g_s.at[j, t, d], g_r.at[j, t, d], {"ctx": to})
            if j == 0:
                g[j, t, 2] = send(
                    block, block, g_s.at[j, t, 2], g_r.at[j, t, 2], {"ctx": across(y)})

    for j in range(4):
        for t in range(2):
            zc = pairs[j][t]

            @pl.loop(0, 2)
            def _(kk):
                rows = rows_of(zc, kk)
                onehot = jnp.where(hits(rows), 1.0, 0.0)
                grad = cc[rows, 0:1] * (onehot - ex[zc, kk] * cc[rows, 1:2])
                ga[zc, y, kk] = grad.astype(BF16)

        if j < AHEAD:
            gather_send(j)
    lg_copies = [
        pltpu.make_async_copy(ga.at[:, y, kk], lg_out.at[kk], out_sem.at[kk]) for kk in range(2)
    ]
    for copy in lg_copies:
        copy.start()

    w_copy.wait_recv()
    x1, x2, cr, cl, dr, dl, gb = {}, {}, {}, {}, {}, {}, {}
    sides = ((0, flip(x), mirror(x), hg_a, xa1, xa2), (1, mirror(x), flip(x), hg_b, xb1, xb2))

    def gather_forward(j):
        for t, zc in enumerate(pairs[j]):
            g[j, t, t].wait_recv()
            origin, to = ((y_left, y_right), (y_right, y_left))[t]
            block = ga.at[zc, origin]
            g[j, t, 2] = send(block, block, g_s.at[j, t, 2], g_r.at[j, t, 2], {"ctx": to})
        if j + 1 < 4:
            gather_send(j + 1)

    def gather_step(j):
        gb[j] = []
        for t, zc in enumerate(pairs[j]):
            if j == 0:
                g[j, t, t].wait_recv()
            g[j, t, 1 - t].wait_recv()
            g[j, t, 2].wait_recv()
            gb[j].append(
                send(ga.at[zc, :, 1 - k], gsib.at[zc], gb_s.at[j, t], gb_r.at[j, t], sib))

    def hidden_grad_step(j):
        for copy in gb[j]:
            copy.wait_recv()
        lhs = jnp.concatenate(
            [
                jnp.concatenate([ga[zc, :, k].reshape(NX * ROWS, vocab) for zc in pairs[j]], axis=0),
                jnp.concatenate([gsib[zc].reshape(NX * ROWS, vocab) for zc in pairs[j]], axis=0),
            ],
            axis=1,
        )
        r = jnp.dot(lhs, wt[:, WA + WB :], preferred_element_type=F32)
        for t in range(2):
            q = r[t * 64 : (t + 1) * 64].reshape(NX, ROWS, 2 * WZ)
            for p in range(2):
                hg_z[j, t, p] = q[:, :, p * WZ : (p + 1) * WZ]
        if j < 3:
            z_first(j)
        for buf, cols in ((hg_a, slice(0, WA)), (hg_b, slice(WA, WA + WB))):
            r = jnp.dot(lhs, wt[:, cols], preferred_element_type=F32)
            for t in range(2):
                buf[j, :, t] = r[t * 64 : (t + 1) * 64].reshape(NX, ROWS, r.shape[1])
        for slot in (1, 0):
            for p, partner, _, buf, first, _ in sides:
                quarter = across(x) if slot else partner
                x1[j, p, slot] = send(
                    buf.at[j, quarter], first.at[j, slot],
                    x1_s.at[j, p, slot], x1_r.at[j, p, slot], {"section": 2 * partner + k})
        if j == 3:
            z_first(j)

    def z_first(j):
        for p in range(2):
            if j > 0:
                dr[j - 1, p].wait_recv()
                hg_z[j, 0, p] = hg_z[j, 0, p] + zz_r[j - 1, p]
            if j < 3:
                dr[j, p] = send(
                    hg_z.at[j, 0, p], zz_r.at[j, p], dr_s.at[j, p], dr_r.at[j, p], z_right)
            if j > 0:
                dl[j - 1, p].wait_recv()
                hg_z[j, 1, p] = hg_z[j, 1, p] + zz_l[j - 1, p]
            dl[j, p] = send(
                hg_z.at[j, 1, p], zz_l.at[j, p], dl_s.at[j, p], dl_r.at[j, p], z_left)

    def x1_take(j):
        for p, _, partner, buf, first, second in sides:
            x1[j, p, 1].wait_recv()
            first[j, 1] = first[j, 1] + buf[j, partner]
            x2[j, p] = send(
                first.at[j, 1], second.at[j], x2_s.at[j, p], x2_r.at[j, p],
                {"section": 2 * partner + k})

    def x2_take(j):
        if j > 0:
            cr[j - 1].wait_recv()
            cl[j - 1].wait_recv()
        for p, _, _, buf, first, second in sides:
            x1[j, p, 0].wait_recv()
            x2[j, p].wait_recv()
            cols = slice(WA, WA + WB) if p else slice(0, WA)
            a, b = [buf[j, x, t] + first[j, 0, t] + second[j, t] for t in range(2)]
            if j > 0:
                a = a + zr_r[j - 1, :, cols]
                b = b + zr_l[j - 1, :, cols]
            zo[j, 0, :, cols] = a
            zo[j, 1, :, cols] = b
        if j < 3:
            cr[j] = send(zo.at[j, 0], zr_r.at[j], cr_s.at[j], cr_r.at[j], z_right)
        cl[j] = send(zo.at[j, 1], zr_l.at[j], cl_s.at[j], cl_r.at[j], z_left)

    e1, e2 = {}, {}

    def z_first_end():
        for p, partner in ((0, flip(x)), (1, mirror(x))):
            dl[3, p].wait_recv()
            hg_z[3, 0, p] = hg_z[3, 0, p] + zz_l[3, p]
            for slot in (1, 0):
                quarter = across(x) if slot else partner
                e1[p, slot] = send(
                    hg_z.at[3, 0, p, quarter], xz1.at[p, slot],
                    e1_s.at[p, slot], e1_r.at[p, slot], {"section": 2 * partner + k})

    def z_first_take():
        for p, partner in ((0, mirror(x)), (1, flip(x))):
            e1[p, 1].wait_recv()
            xz1[p, 1] = xz1[p, 1] + hg_z[3, 0, p, partner]
            e2[p] = send(
                xz1.at[p, 1], xz2.at[p], e2_s.at[p], e2_r.at[p], {"section": 2 * partner + k})

    w_copies = []

    def weight_grad_step(i):
        rows = slice(i * 512, (i + 1) * 512)
        tokens = hid[:, :, :, :, rows].reshape(NZ * NX * 2 * ROWS, 512)
        grads = ga[...].reshape(NZ * NY * 2 * ROWS, vocab)
        r = lax.dot_general(tokens, grads, (((0,), (0,)), ((), ())), preferred_element_type=F32)
        wst[i] = r.astype(BF16)
        copy = pltpu.make_async_copy(wst.at[i], wg_out.at[i], out_sem.at[2 + i])
        copy.start()
        w_copies.append(copy)

    for j in range(4):
        gather_step(j)
        if j < 3:
            gather_forward(j + 1)
        if j >= 1:
            x1_take(j - 1)
        hidden_grad_step(j)
        if j >= 2:
            x2_take(j - 2)
    weight_grad_step(0)
    x1_take(3)
    weight_grad_step(1)
    x2_take(2)
    z_first_end()
    weight_grad_step(2)
    x2_take(3)
    z_first_take()
    weight_grad_step(3)
    cl[3].wait_recv()
    hg_out[:, : WA + WB] = (zo[3, 0] + zr_l[3]).astype(BF16)
    for p in range(2):
        e1[p, 0].wait_recv()
        e2[p].wait_recv()
        cols = slice(WA + WB + p * WZ, WA + WB + (p + 1) * WZ)
        hg_out[:, cols] = (hg_z[3, 0, p, x] + xz1[p, 0] + xz2[p]).astype(BF16)
    for copy in lg_copies + w_copies:
        copy.wait()
    for copy in sends:
        copy.wait_send()


def finish(lp_in, lg_in, wg_in, hg_in, lp_out, lg_out, wg_out, hg_out, lp_buf, lg_buf, wg_buf, hg_buf, in_sem, out_sem):
    blocks = [(wg_in, wg_buf, wg_out, i) for i in range(16)]
    blocks += [(lg_in, lg_buf, lg_out, i) for i in range(4)]
    blocks += [(lp_in, lp_buf, lp_out, 0), (hg_in, hg_buf, hg_out, 0)]
    reads = [
        pltpu.make_async_copy(src.at[i], buf.at[i], in_sem.at[n])
        for n, (src, buf, _, i) in enumerate(blocks)
    ]
    writes = [
        pltpu.make_async_copy(buf.at[i], dst.at[i], out_sem.at[n])
        for n, (_, buf, dst, i) in enumerate(blocks)
    ]
    for copy in reads:
        copy.start()
    for read, write in zip(reads, writes):
        read.wait()
        write.start()
    for copy in writes:
        copy.wait()


def shards(hidden, head_weight, target_ids, seq_ids, response_mask, ref_means):
    rows, width = hidden.shape
    vocab = head_weight.shape[1]
    tokens = target_ids.shape[0]
    dma = pltpu.SemaphoreType.DMA
    anywhere, vmem = pl.BlockSpec(memory_space=pl.ANY), pl.BlockSpec(memory_space=pltpu.VMEM)
    lp, lg, wg, hg = pl.pallas_call(
        kernel,
        out_shape=(
            jax.ShapeDtypeStruct((1, tokens), F32),
            jax.ShapeDtypeStruct((2, NZ, ROWS, vocab), BF16),
            jax.ShapeDtypeStruct((4, width // 4, vocab), BF16),
            jax.ShapeDtypeStruct((rows, width), BF16),
        ),
        in_specs=[anywhere, anywhere, vmem, vmem, vmem, pl.BlockSpec(memory_space=pltpu.SMEM)],
        out_specs=(vmem, anywhere, anywhere, vmem),
        scratch_shapes=[
            pltpu.VMEM((NZ, NX, 2, ROWS, width), BF16),
            pltpu.VMEM((width, vocab), BF16),
            pltpu.VMEM((2 * vocab, width), BF16),
            pltpu.VMEM((NZ, 2, NY, 2, ROWS, vocab // 2), F32),
            pltpu.VMEM((NZ, 2, 2, 2, ROWS, vocab // 2), F32),
            pltpu.VMEM((NZ, 2, 2, ROWS, vocab // 2), F32),
            pltpu.VMEM((NZ, 2, ROWS, vocab), F32),
            pltpu.VMEM((tokens, 128), F32),
            pltpu.VMEM((tokens, 128), F32),
            pltpu.VMEM((tokens, 128), F32),
            pltpu.VMEM((8, 8, tokens), F32),
            pltpu.VMEM((NZ, 8, tokens), F32),
            pltpu.VMEM((NY, 8, 128), F32),
            pltpu.VMEM((NZ, NY, 2, ROWS, vocab), BF16),
            pltpu.VMEM((NZ, NY, ROWS, vocab), BF16),
            pltpu.VMEM((4, NX, 2, ROWS, WA), F32),
            pltpu.VMEM((4, NX, 2, ROWS, WB), F32),
            pltpu.VMEM((4, 2, 2, NX, ROWS, WZ), F32),
            pltpu.VMEM((4, 2, 2, ROWS, WA), F32),
            pltpu.VMEM((4, 2, 2, ROWS, WB), F32),
            pltpu.VMEM((4, 2, ROWS, WA), F32),
            pltpu.VMEM((4, 2, ROWS, WB), F32),
            pltpu.VMEM((4, 2, ROWS, WA + WB), F32),
            pltpu.VMEM((3, ROWS, WA + WB), F32),
            pltpu.VMEM((4, ROWS, WA + WB), F32),
            pltpu.VMEM((3, 2, NX, ROWS, WZ), F32),
            pltpu.VMEM((4, 2, NX, ROWS, WZ), F32),
            pltpu.VMEM((2, 2, ROWS, WZ), F32),
            pltpu.VMEM((2, ROWS, WZ), F32),
            pltpu.VMEM((4, width // 4, vocab), BF16),
            dma((2,)),
            dma((8, 3)), dma((8, 3)), dma((7,)), dma((7,)), dma((8,)), dma((8,)),
            dma, dma,
            dma((8, 2, 2)), dma((8, 2, 2)), dma((8, 2)), dma((8, 2)),
            dma((7,)), dma((7,)), dma((7,)), dma((7,)), dma((3,)), dma((3,)),
            dma((4, 2, 3)), dma((4, 2, 3)), dma((4, 2)), dma((4, 2)),
            dma((4, 2, 2)), dma((4, 2, 2)), dma((4, 2)), dma((4, 2)),
            dma((3,)), dma((3,)), dma((4,)), dma((4,)),
            dma((3, 2)), dma((3, 2)), dma((4, 2)), dma((4, 2)),
            dma((2, 2)), dma((2, 2)), dma((2,)), dma((2,)),
            dma((6,)),
        ],
        compiler_params=pltpu.CompilerParams(
            collective_id=0, has_side_effects=True, vmem_limit_bytes=56 * 1024 * 1024),
    )(
        hidden, head_weight,
        target_ids.reshape(1, tokens), seq_ids.reshape(1, tokens), response_mask.reshape(1, tokens),
        ref_means,
    )
    lg, wg = lg.reshape(4, tokens // 4, vocab), wg.reshape(16, width // 16, vocab)
    lp, hg = lp.reshape(1, 1, tokens), hg.reshape(1, rows, width)
    lp, lg, wg, hg = pl.pallas_call(
        finish,
        out_shape=tuple(jax.ShapeDtypeStruct(v.shape, v.dtype) for v in (lp, lg, wg, hg)),
        in_specs=[anywhere] * 4,
        out_specs=(anywhere,) * 4,
        scratch_shapes=[
            pltpu.VMEM(lp.shape, F32), pltpu.VMEM(lg.shape, BF16),
            pltpu.VMEM(wg.shape, BF16), pltpu.VMEM(hg.shape, BF16),
            dma((22,)), dma((22,)),
        ],
        compiler_params=pltpu.CompilerParams(vmem_limit_bytes=56 * 1024 * 1024),
    )(lp, lg, wg, hg)
    return (
        lp.reshape(tokens), lg.reshape(tokens, vocab), wg.reshape(width, vocab),
        hg.reshape(rows, width),
    )


def solution(mesh):
    in_specs = (
        P(("section", "tensor"), "ctx"),
        P("ctx", ("section", "tensor")),
        P("ctx"),
        P("ctx"),
        P("ctx"),
        P(),
    )
    out_specs = (
        P("ctx"),
        P("ctx", ("section", "tensor")),
        P("ctx", ("section", "tensor")),
        P(("section", "tensor"), "ctx"),
    )
    return jax.shard_map(shards, mesh=mesh, in_specs=in_specs, out_specs=out_specs, check_vma=False)
```
